128 devices in a mesh: ckpt: 8 (over y_hi, x), row: 16 (over y_lo, z, core).
Axes of the slice: x: 4, y: 4 (y_hi: 2, y_lo: 2; y = y_hi * 2 + y_lo), z: 4, core: 2. Of those that a mesh axis runs over, the one named last changes fastest.
Arguments:
- quant_codes: bfloat16 [8, 16384, 8192], P('ckpt', 'row'), may hold values from -127 to 127, as said below
- exponents: int32 [8, 128, 64], P('ckpt', 'row'), may hold values from -8 to -4
- numerators: int32 [8], replicated, may hold values from 1 to 9
- denominator: int32 [1], replicated, may hold values from 16 to 64
Outputs:
- block_tiles: bfloat16 [16384, 8192], P('ckpt', 'row')
- block_scales: float32 [128, 64], P('ckpt', 'row')
The draws below stay inside these ranges and needn't reach their ends.
Inputs may be any that keep to these rules, and one draw needn't show every extreme that they name: `quant_codes`: every entry is a whole number.
All inputs are finite; a program needn't handle non-finite values. Where the reference program divides by a largest or mean magnitude, that divisor is 1e-20 or more.
Results may differ from the reference program's by a relative error of at most 0.001.
Values may be sent and summed in bfloat16 or wider, within the bound.
No kernel may reach another device: no remote copies, remote signals or barrier semaphores. Data moves between devices by JAX's collectives and lax.ppermute only.
A program may use at most 256 MiB of HBM per device.

```python
import jax
import jax.numpy as jnp
from jax import lax

D = 8192
ROWS = 16384
BLOCK = 128
CKPTS = 8


def draw_quant_codes(key, part):
    key = jax.random.fold_in(key, 11)
    keys = jax.random.split(key, 4)
    row_scale = jnp.exp(jax.random.uniform(keys[0], (ROWS, 1), jnp.float32, -2.3026, 0.0))
    col_scale = jnp.exp(jax.random.uniform(keys[1], (1, D), jnp.float32, -2.3026, 0.0))
    shared = jax.random.normal(keys[2], (ROWS, D), jnp.float32)
    noise_part = jax.random.normal(keys[3], (CKPTS, ROWS, D), jnp.float32)
    mixed = 48.0 * (0.5 * shared + 0.87 * noise_part)
    raw_values = mixed * row_scale * col_scale
    return jnp.clip(jnp.floor(raw_values + 0.5), -127.0, 127.0).astype(jnp.bfloat16)


def with_ends(entries, stream_key, low, high):
    index_at = [jax.random.randint(jax.random.fold_in(stream_key, axis), (), 0, length) for axis, length in enumerate(entries.shape)]
    widest = entries.shape.index(max(entries.shape))
    beside = index_at[:widest] + [(index_at[widest] + 1) % entries.shape[widest]] + index_at[widest + 1:]
    return entries.at[tuple(index_at)].set(low).at[tuple(beside)].set(high)


def setup_inputs(seed: int = 0) -> dict:
    arg_keys = jax.random.split(jax.random.key(seed), 5)
    return {
        "quant_codes": draw_quant_codes(jax.random.fold_in(arg_keys[4], 71), 0),
        "exponents": with_ends(jax.random.randint(arg_keys[1], (CKPTS, ROWS // BLOCK, D // BLOCK), -8, -3), jax.random.fold_in(arg_keys[1], 1), -8, (-3) - 1).astype(jnp.int32),
        "numerators": with_ends(jax.random.randint(arg_keys[2], (CKPTS,), 1, 10), jax.random.fold_in(arg_keys[2], 1), 1, 9).astype(jnp.int32),
        "denominator": jax.random.randint(arg_keys[3], (1,), 16, 65).astype(jnp.int32),
    }


epsilon = 1e-6


def reference(quant_codes, exponents, numerators, denominator):
    row_count = quant_codes.shape[1]
    col_count = quant_codes.shape[2]

    def accumulate(index, summed):
        slab_codes = lax.dynamic_index_in_dim(quant_codes, index, 0, keepdims=False).astype(jnp.float32)
        slab_codes = slab_codes.reshape(row_count // BLOCK, BLOCK, col_count // BLOCK, BLOCK)
        powers_block = jnp.exp2(lax.dynamic_index_in_dim(exponents, index, 0, keepdims=False).astype(jnp.float32))
        weight_value = lax.dynamic_index_in_dim(numerators, index, 0, keepdims=False).astype(jnp.float32)
        return summed + weight_value * (slab_codes * powers_block[:, None, :, None])

    start_sum = jnp.zeros((row_count // BLOCK, BLOCK, col_count // BLOCK, BLOCK), jnp.float32)
    summed = lax.fori_loop(0, CKPTS, accumulate, start_sum)
    average = summed / denominator[0].astype(jnp.float32)
    block_scales = jnp.max(jnp.abs(average), axis=(1, 3))
    block_tiles = average / (block_scales + epsilon)[:, None, :, None]
    return block_tiles.reshape(row_count, col_count).astype(jnp.bfloat16), block_scales
```

```python
import jax
import jax.numpy as jnp
from jax import lax
from jax.experimental import pallas as pl
from jax.experimental.pallas import tpu as pltpu
from jax.sharding import PartitionSpec as P

BLOCK = 128
EPSILON = 1e-6
AXES = ("ckpt", "row")
OWN, PARTNER, KEEP, YHI, SHIFT, FLIP = range(6)
TILE_COLS = 512
CHUNK = 256
CHUNKS = 1024 // CHUNK
BANDS = CHUNK // BLOCK
EXTRA = CHUNK // 16
SPAN = TILE_COLS // BLOCK


def device_index(x, y, z, core):
    y_hi, y_lo = divmod(y, 2)
    return (y_hi * 4 + x) * 16 + y_lo * 8 + z * 2 + core


def permutation(target):
    return [
        (device_index(x, y, z, core), device_index(*target(x, y, z, core)))
        for x in range(4)
        for y in range(4)
        for z in range(4)
        for core in range(2)
    ]


def pair_of(x, core):
    return x + 1 - 2 * ((x + core) % 2)


ACROSS = {0: 1, 1: 3, 2: 0, 3: 2}
BESIDE = {0: 0, 1: 2, 2: 1, 3: 3}
PAIR_PERM = permutation(lambda x, y, z, core: (pair_of(x, core) % 4, y, z, core))
ACROSS_PERM = permutation(lambda x, y, z, core: (x, ACROSS[y], z, core))
BESIDE_PERM = permutation(lambda x, y, z, core: (x, BESIDE[y], z, core))
Z_PERMS = [permutation(lambda x, y, z, core, m=m: (x, y, (z - x - m) % 4, core)) for m in range(4)]
X_PERMS = [
    permutation(lambda x, y, z, core, m=m: ((x + z + m) % 4, y, z, core ^ (x % 2))) for m in range(4)
]
ZX_PERMS = [
    permutation(lambda x, y, z, core, m=m: (z, y, (z - x - m) % 4, core ^ (x % 2))) for m in range(4)
]


def call(kernel, grid, scalars, inputs, outputs, after=()):
    held = len(after)

    def whole(*refs):
        kernel(*refs[: len(scalars) + len(inputs)], *refs[len(scalars) + len(inputs) + held :])

    moved = sum(a.dtype.itemsize * a.size for a, _, _ in inputs) + sum(
        jnp.dtype(d).itemsize * s[0] * s[1] for s, d, _, _ in outputs
    )
    return pl.pallas_call(
        whole,
        grid_spec=pltpu.PrefetchScalarGridSpec(
            num_scalar_prefetch=len(scalars),
            grid=grid,
            in_specs=[pl.BlockSpec(b, m) for _, b, m in inputs] + [pl.BlockSpec(memory_space=pl.ANY)] * held,
            out_specs=[pl.BlockSpec(b, m) for _, _, b, m in outputs],
        ),
        out_shape=[jax.ShapeDtypeStruct(s, d) for s, d, _, _ in outputs],
        compiler_params=pltpu.CompilerParams(vmem_limit_bytes=40 * 1024 * 1024),
        cost_estimate=pl.CostEstimate(flops=0, bytes_accessed=moved, transcendentals=0),
    )(*scalars, *[a for a, _, _ in inputs], *after)


def block_of(band, col):
    return pl.ds(band * BLOCK, BLOCK), pl.ds(col * BLOCK, BLOCK)


def pack(chunk, place, codes, after):
    def kernel(place, codes, sent):
        sent[...] = codes[0]

    return call(
        kernel,
        (8,),
        [place],
        [(codes, (1, CHUNK, TILE_COLS), lambda j, place: (0, chunk, 2 * j + 1 - place[KEEP]))],
        [((CHUNK, 8 * TILE_COLS), jnp.bfloat16, (CHUNK, TILE_COLS), lambda j, place: (0, j))],
        after,
    )[0]


def add_pairs(chunk, place, weights, own_exps, partner_exps, codes, received):
    def kernel(place, weights, own_exps, partner_exps, c_far, c_near, r_far, r_near, far, near):
        own_weight, partner_weight = weights[place[OWN]], weights[place[PARTNER]]
        z_to = pl.program_id(0)
        for y_lo, kept, came, out in (
            (1 - place[YHI], c_far, r_far, far),
            (place[YHI], c_near, r_near, near),
        ):
            first = (y_lo * 8 + z_to * 2 + place[KEEP]) * SPAN
            for band in range(BANDS):
                for col in range(SPAN):
                    own = own_exps[chunk * BANDS + band, first + col]
                    partner = partner_exps[chunk * BANDS + band, first + col]
                    unit = jnp.minimum(own, partner)
                    own_scale = (own_weight << (own - unit)).astype(jnp.float32)
                    partner_scale = (partner_weight << (partner - unit)).astype(jnp.float32)
                    rows, cols = block_of(band, col)
                    total = (
                        kept[0, rows, cols].astype(jnp.float32) * own_scale
                        + came[rows, cols].astype(jnp.float32) * partner_scale
                    )
                    out[rows, cols] = total.astype(jnp.int32).astype(jnp.int16)

    block = (CHUNK, TILE_COLS)
    kept_block = (1, CHUNK, TILE_COLS)
    return call(
        kernel,
        (4,),
        [place, weights, own_exps, partner_exps],
        [
            (codes, kept_block, lambda t, p, *_: (0, chunk, 2 * ((1 - p[YHI]) * 4 + t) + p[KEEP])),
            (codes, kept_block, lambda t, p, *_: (0, chunk, 2 * (p[YHI] * 4 + t) + p[KEEP])),
            (received, block, lambda t, p, *_: (0, (1 - p[YHI]) * 4 + t)),
            (received, block, lambda t, p, *_: (0, p[YHI] * 4 + t)),
        ],
        [((CHUNK, 4 * TILE_COLS), jnp.int16, block, lambda t, *_: (0, t))] * 2,
    )


def add_fours(chunk, place, far_units, near_units, far, near):
    def kernel(place, far_units, near_units, far, near, *outs):
        z_to = lax.rem(place[SHIFT] + 4 - pl.program_id(0), 4)
        y_lo = place[YHI + 0]
        first = (place[6] * 8 + z_to * 2 + place[KEEP]) * SPAN
        for slot, out in enumerate(outs):

            @pl.when(pl.program_id(0) == slot)
            def _():
                for col in range(SPAN):
                    odds = []
                    for band in range(BANDS):
                        far_unit = far_units[chunk * BANDS + band, first + col]
                        near_unit = near_units[chunk * BANDS + band, first + col]
                        unit = jnp.minimum(far_unit, near_unit)
                        rows, cols = block_of(band, col)
                        total = (far[rows, cols].astype(jnp.int32) << (far_unit - unit)) + (
                            near[rows, cols].astype(jnp.int32) << (near_unit - unit)
                        )
                        out[rows, cols] = (total >> 1).astype(jnp.int16)
                        odd = total & 1
                        packed = odd[0:8]
                        for group in range(1, 16):
                            packed = packed | (odd[8 * group : 8 * group + 8] << group)
                        odds.append(packed)
                    out[pl.ds(CHUNK, EXTRA), pl.ds(col * BLOCK, BLOCK)] = jnp.concatenate(
                        odds, axis=0
                    ).astype(jnp.int16)

    block = (CHUNK, TILE_COLS)
    sent = (CHUNK + EXTRA, TILE_COLS)
    z_block = lambda t, p, *_: (0, lax.rem(p[SHIFT] + 4 - t, 4))
    return call(
        kernel,
        (4,),
        [place, far_units, near_units],
        [(far, block, z_block), (near, block, z_block)],
        [(sent, jnp.int16, sent, lambda t, *_: (0, 0))] * 4,
    )


def finish(place, denominator, units, parts):
    def kernel(place, denominator, *refs):
        units, refs = refs[:4], refs[4:]
        parts, (tiles, scales) = refs[: 4 * CHUNKS], refs[4 * CHUNKS :]
        chunk, half = pl.program_id(0), pl.program_id(1)
        divisor = jnp.full((1, 1), denominator[0], jnp.int32).astype(jnp.float32)
        core_rows = lax.rem(place[FLIP] + half, 2)
        first = place[7] * SPAN

        def fours(ref, unit, band, col):
            rows, cols = block_of(band, col)
            packed = ref[pl.ds(CHUNK, EXTRA), cols].astype(jnp.int32)[8 * band : 8 * band + 8]
            odd = jnp.concatenate([(packed >> group) & 1 for group in range(16)], axis=0)
            total = (ref[rows, cols].astype(jnp.int32) << 1) + odd
            return total.astype(jnp.float32) * ((1 << (unit + 8)).astype(jnp.float32) * (1.0 / 256))

        @pl.when((chunk == 0) & (half == 0))
        def _():
            scales[...] = jnp.zeros_like(scales)

        row_at = lax.broadcasted_iota(jnp.int32, scales.shape, 0)
        col_at = lax.broadcasted_iota(jnp.int32, scales.shape, 1)
        for c in range(CHUNKS):
            for h in range(2):

                @pl.when((chunk == c) & (half == h))
                def _():
                    found = scales[...]
                    for band in range(BANDS):
                        for col in range(SPAN):
                            at = (c * BANDS + band, first + col)
                            summed = fours(parts[4 * c + h], units[h][at], band, col) + fours(
                                parts[4 * c + h + 2], units[h + 2][at], band, col
                            )
                            largest = jnp.max(jnp.abs(summed), axis=(0, 1), keepdims=True)
                            scale = largest / divisor
                            rows, cols = block_of(band, col)
                            factor = 1.0 / (divisor * (scale + EPSILON))
                            tiles[rows, cols] = (summed * factor).astype(jnp.bfloat16)
                            here = (row_at == core_rows * 8 + c * BANDS + band) & (col_at == col)
                            found = jnp.where(here, scale, found)
                    scales[...] = found

    sent = (CHUNK + EXTRA, TILE_COLS)
    return call(
        kernel,
        (CHUNKS, 2),
        [place, denominator, *units],
        [(part, sent, lambda c, h, *_: (0, 0)) for part in parts],
        [
            (
                (2048, TILE_COLS),
                jnp.bfloat16,
                (CHUNK, TILE_COLS),
                lambda c, h, p, *_: (lax.rem(p[FLIP] + h, 2) * CHUNKS + c, 0),
            ),
            ((16, 4), jnp.float32, (16, 4), lambda c, h, *_: (0, 0)),
        ],
    )


def body(quant_codes, exponents, numerators, denominator):
    y_hi, x = jnp.divmod(lax.axis_index("ckpt"), 4)
    row = lax.axis_index("row")
    y_lo, z, core = row // 8, (row // 2) % 4, row % 2
    keep = (x + core) % 2
    place = jnp.stack(
        [
            y_hi * 4 + x,
            y_hi * 4 + (x + 1 - 2 * keep) % 4,
            keep,
            y_hi,
            (z - x) % 4,
            (x - z - core) % 2,
            y_lo,
            row,
        ]
    ).astype(jnp.int32)

    own_exps = exponents[0]
    partner_exps = lax.ppermute(own_exps, AXES, PAIR_PERM)
    pair_units = jnp.minimum(own_exps, partner_exps)
    far_units = lax.ppermute(pair_units, AXES, ACROSS_PERM)
    near_units = lax.ppermute(pair_units, AXES, BESIDE_PERM)
    four_units = jnp.minimum(far_units, near_units)
    units = [lax.ppermute(four_units, AXES, perm) for perm in ZX_PERMS]

    parts = []
    after = ()
    for chunk in range(CHUNKS):
        sent = pack(chunk, place, quant_codes, after)
        received = lax.ppermute(sent, AXES, PAIR_PERM)
        after = (received,)
        far, near = add_pairs(chunk, place, numerators, own_exps, partner_exps, quant_codes, received)
        far = lax.ppermute(far, AXES, ACROSS_PERM)
        near = lax.ppermute(near, AXES, BESIDE_PERM)
        slots = add_fours(chunk, place, far_units, near_units, far, near)
        slots = [lax.ppermute(slot, AXES, perm) for slot, perm in zip(slots, Z_PERMS)]
        slots = [lax.ppermute(slot, AXES, perm) for slot, perm in zip(slots, X_PERMS)]
        parts += slots
    return tuple(finish(place, denominator, units, parts))


def solution(mesh):
    placed = (P("ckpt", "row", None), P("ckpt", "row", None), P(), P())
    return jax.shard_map(
        body,
        mesh=mesh,
        in_specs=placed,
        out_specs=(P("ckpt", "row"), P("ckpt", "row")),
        check_vma=False,
    )
```

```python
import jax
import jax.numpy as jnp
from jax import lax
from jax.experimental import pallas as pl
from jax.experimental.pallas import tpu as pltpu
from jax.sharding import PartitionSpec as P

BLOCK = 128
EPSILON = 1e-6
AXES = ("ckpt", "row")
OWN, PARTNER, KEEP, YHI, SLOT, CORE = range(6)
TILE = 512
ROWS = 1024
CHUNK = 256
CHUNKS = ROWS // CHUNK
BANDS = CHUNK // BLOCK
BITS = CHUNK // 16
LAST = CHUNKS - 1
UNITS = 16


def device_index(x, y, z, core):
    y_hi, y_lo = divmod(y, 2)
    return (y_hi * 4 + x) * 16 + y_lo * 8 + z * 2 + core


def permutation(target):
    return [
        (device_index(x, y, z, core), device_index(*target(x, y, z, core)))
        for x in range(4)
        for y in range(4)
        for z in range(4)
        for core in range(2)
    ]


def pair_of(x, y, z, core):
    return (x + 1 - 2 * ((x + core) % 2)) % 4, y, z, core


def z_target(m, x, y, z, core):
    away = (z - x) % 4
    return x, y, (x + core) % 2 + 2 * (m ^ (away // 2)), away % 2


def x_target(m, x, y, z, core):
    return (x + core + 2 * (m ^ (z // 2))) % 4, y, z, (z - x) % 2


ACROSS = {0: 1, 1: 3, 2: 0, 3: 2}
BESIDE = {0: 0, 1: 2, 2: 1, 3: 3}
PAIR_PERM = permutation(pair_of)
ACROSS_PERM = permutation(lambda x, y, z, core: (x, ACROSS[y], z, core))
BESIDE_PERM = permutation(lambda x, y, z, core: (x, BESIDE[y], z, core))
Z_PERMS = [permutation(lambda *at, m=m: z_target(m, *at)) for m in range(2)]
X_PERMS = [permutation(lambda *at, m=m: x_target(m, *at)) for m in range(2)]
CORE_PERM = permutation(lambda x, y, z, core: (x, y, z, 1 - core))


def call(kernel, grid, scalars, inputs, outputs, after=(), scratch=(), aliases=None):
    first = len(scalars) + len(inputs)

    def whole(*refs):
        kernel(*refs[:first], *refs[first + len(after) :])

    moved = sum(a.dtype.itemsize * a.size for a, _ in inputs)
    return pl.pallas_call(
        whole,
        grid_spec=pltpu.PrefetchScalarGridSpec(
            num_scalar_prefetch=len(scalars),
            grid=grid,
            in_specs=[spec for _, spec in inputs] + [pl.BlockSpec(memory_space=pl.ANY)] * len(after),
            out_specs=[spec for _, _, spec in outputs],
            scratch_shapes=scratch,
        ),
        out_shape=[jax.ShapeDtypeStruct(s, d) for s, d, _ in outputs],
        input_output_aliases=aliases or {},
        compiler_params=pltpu.CompilerParams(vmem_limit_bytes=40 * 1024 * 1024),
        cost_estimate=pl.CostEstimate(flops=0, bytes_accessed=moved, transcendentals=0),
    )(*scalars, *[a for a, _ in inputs], *after)


def later(values, *after):
    return lax.optimization_barrier((tuple(values), after))[0] if after else values


ANYWHERE = pl.BlockSpec(memory_space=pl.ANY)


def pack(chunk, place, codes, wide_exps, after):
    extra = UNITS if chunk == 0 else 0

    def kernel(place, codes, wide_exps, sent, sems):
        copies = []
        for group in range(4):
            y_lo, t = divmod(group, 2)
            first = pl.multiple_of((y_lo * 4 + 1 - place[KEEP] + 2 * t) * 2 * TILE, BLOCK)
            cols, to = pl.ds(first, 2 * TILE), pl.ds(group * 2 * TILE, 2 * TILE)
            copies.append(
                pltpu.make_async_copy(
                    codes.at[0, pl.ds(chunk * CHUNK, CHUNK), cols],
                    sent.at[pl.ds(0, CHUNK), to],
                    sems.at[group],
                )
            )
            if extra:
                copies.append(
                    pltpu.make_async_copy(
                        wide_exps.at[:, cols], sent.at[pl.ds(CHUNK, UNITS), to], sems.at[4 + group]
                    )
                )
        for copy in copies:
            copy.start()
        for copy in copies:
            copy.wait()

    return call(
        kernel,
        (),
        [place],
        [(codes, ANYWHERE), (wide_exps, ANYWHERE)],
        [((CHUNK + extra, 8 * TILE), jnp.bfloat16, ANYWHERE)],
        after,
        [pltpu.SemaphoreType.DMA((8,))],
    )[0]


def whole_number(ref):
    return ref[...].astype(jnp.float32).astype(jnp.int32)


def add_pairs(chunk, place, weights, wide_exps, codes, first_received, received, after):
    extra = UNITS if chunk == 0 else 0

    def kernel(place, weights, *refs):
        own_weight, partner_weight = weights[place[OWN]], weights[place[PARTNER]]
        for at in range(2):
            kept, came, own, partner, out = refs[at::2]
            own, partner = whole_number(own), whole_number(partner)
            unit = jnp.minimum(own, partner)
            own = (jnp.full(own.shape, own_weight, jnp.int32) << (own - unit)).astype(jnp.float32)
            partner = (jnp.full(own.shape, partner_weight, jnp.int32) << (partner - unit)).astype(
                jnp.float32
            )
            for band in range(BANDS):
                row = chunk * BANDS + band
                rows = pl.ds(band * BLOCK, BLOCK)
                for col in range(TILE // BLOCK):
                    cols = slice(col * BLOCK, (col + 1) * BLOCK)
                    total = (
                        kept[0, rows, cols].astype(jnp.float32) * own[row : row + 1, cols]
                        + came[rows, cols].astype(jnp.float32) * partner[row : row + 1, cols]
                    )
                    out[rows, cols] = total.astype(jnp.int32).astype(jnp.int16)
            if extra:
                out[pl.ds(CHUNK, UNITS), :] = unit.astype(jnp.int16)

    def kept_col(y_lo, t):
        return lambda p: 2 * (y_lo(p) * 4 + p[KEEP] + 2 * (t // 2)) + t % 2

    far, near = (lambda p: 1 - p[YHI]), (lambda p: p[YHI])

    def kept_at(y_lo, row):
        return lambda t, p, w: (*row, 2 * (y_lo(p) * 4 + p[KEEP] + 2 * (t // 2)) + t % 2)

    def came_at(y_lo, row):
        return lambda t, p, w: (row, y_lo(p) * 4 + t)

    sent = (CHUNK + extra, TILE)
    return call(
        kernel,
        (4,),
        [place, weights],
        [(codes, pl.BlockSpec((1, CHUNK, TILE), kept_at(y, (0, chunk)))) for y in (far, near)]
        + [(received, pl.BlockSpec((CHUNK, TILE), came_at(y, 0))) for y in (far, near)]
        + [(wide_exps, pl.BlockSpec((UNITS, TILE), kept_at(y, (0,)))) for y in (far, near)]
        + [(first_received, pl.BlockSpec((UNITS, TILE), came_at(y, CHUNK // UNITS))) for y in (far, near)],
        [((CHUNK + extra, 4 * TILE), jnp.int16, pl.BlockSpec(sent, lambda t, *_: (0, t)))] * 2,
        after,
    )


def add_fours(chunk, place, first_far, first_near, far, near, after):
    extra = UNITS if chunk == 0 else 0

    def kernel(place, far, near, far_unit, near_unit, *outs):
        far_unit, near_unit = far_unit[...].astype(jnp.int32), near_unit[...].astype(jnp.int32)
        unit = jnp.minimum(far_unit, near_unit)
        far_unit, near_unit = far_unit - unit, near_unit - unit

        def fill(out):
            for col in range(2 * TILE // BLOCK):
                cols = slice(col * BLOCK, (col + 1) * BLOCK)
                odds = []
                for band in range(BANDS):
                    row = chunk * BANDS + band
                    rows = pl.ds(band * BLOCK, BLOCK)
                    total = (
                        far[rows, cols].astype(jnp.int32)
                        << jnp.broadcast_to(far_unit[row : row + 1, cols], (BLOCK, BLOCK))
                    ) + (
                        near[rows, cols].astype(jnp.int32)
                        << jnp.broadcast_to(near_unit[row : row + 1, cols], (BLOCK, BLOCK))
                    )
                    out[rows, cols] = (total >> 1).astype(jnp.int16)
                    odd = total & 1
                    packed = odd[0:8]
                    for group in range(1, 16):
                        packed = packed | (odd[8 * group : 8 * group + 8] << group)
                    odds.append(packed)
                out[pl.ds(CHUNK, BITS), cols] = jnp.concatenate(odds, axis=0).astype(jnp.int16)
            if extra:
                out[pl.ds(CHUNK + BITS, UNITS), :] = unit.astype(jnp.int16)

        for slot, out in enumerate(outs):
            pl.when(pl.program_id(0) == slot)(lambda out=out: fill(out))

    rows = CHUNK + BITS + extra
    picked = lambda t, p: jnp.bitwise_xor(t, p[SLOT])
    block = pl.BlockSpec((CHUNK, 2 * TILE), lambda t, p: (0, picked(t, p)))
    units = pl.BlockSpec((UNITS, 2 * TILE), lambda t, p: (CHUNK // UNITS, picked(t, p)))
    return call(
        kernel,
        (2,),
        [place],
        [(far, block), (near, block), (first_far, units), (first_near, units)],
        [((rows, 2 * TILE), jnp.int16, pl.BlockSpec((rows, 2 * TILE), lambda t, p: (0, 0)))] * 2,
        after,
    )


def finish(chunk, place, denominator, first_parts, parts, before):
    chunks, row0 = (1, 0) if chunk == LAST else (CHUNKS - 1, chunk)
    per_half = BANDS * (TILE // BLOCK)

    def kernel(place, denominator, *refs):
        parts, units = refs[:2], refs[2:4]
        old_scales = refs[4] if before else None
        mine, other, scales, summed, factors = refs[-5:]
        core = place[CORE]
        divisor = jnp.full((1, 1), denominator[0], jnp.int32).astype(jnp.float32)
        units = [
            (1 << (unit[...].astype(jnp.int32) + 8)).astype(jnp.float32) * (1.0 / 256) for unit in units
        ]

        def fours(ref, unit, band, cols):
            packed = ref[pl.ds(CHUNK, BITS), cols].astype(jnp.int32)[8 * band : 8 * band + 8]
            odd = jnp.concatenate([(packed >> group) & 1 for group in range(16)], axis=0)
            total = (ref[pl.ds(band * BLOCK, BLOCK), cols].astype(jnp.int32) << 1) + odd
            row = chunk * BANDS + band
            return total.astype(jnp.float32) * unit[row : row + 1, cols]

        blocks = [(h, band, col) for h in range(2) for band in range(BANDS) for col in range(TILE // BLOCK)]
        tops = []
        for half, band, col in blocks:
            cols = slice(half * TILE + col * BLOCK, half * TILE + (col + 1) * BLOCK)
            total = fours(parts[0], units[0], band, cols) + fours(parts[1], units[1], band, cols)
            summed[half, pl.ds(band * BLOCK, BLOCK), col * BLOCK : (col + 1) * BLOCK] = total
            tops.append(jnp.max(jnp.abs(total), axis=0, keepdims=True))
        scale = jnp.max(jnp.concatenate(tops, axis=0), axis=1, keepdims=True) / divisor
        factors[...] = jnp.broadcast_to(1.0 / (divisor * (scale + EPSILON)), factors.shape)
        found = old_scales[...] if before else jnp.zeros_like(scales)
        row_at = lax.broadcasted_iota(jnp.int32, scales.shape, 0)
        col_at = lax.broadcasted_iota(jnp.int32, scales.shape, 1)
        for at, (half, band, col) in enumerate(blocks):
            here = (row_at == chunk * BANDS + band) & (col_at == half * (TILE // BLOCK) + col)
            found = jnp.where(here, scale[at : at + 1, :], found)
        scales[...] = found
        for half, out in ((core, mine), (1 - core, other)):
            for at in range(per_half):
                band, col = divmod(at, TILE // BLOCK)
                rows, cols = pl.ds(band * BLOCK, BLOCK), slice(col * BLOCK, (col + 1) * BLOCK)
                factor = factors[pl.ds(half * per_half + at, 1), :]
                out[rows, cols] = (summed[half, rows, cols] * factor).astype(jnp.bfloat16)

    small = pl.BlockSpec((8, 8), lambda t, *_: (0, 0))
    units = pl.BlockSpec((UNITS, 2 * TILE), lambda t, *_: ((CHUNK + BITS) // UNITS, 0))
    inputs = [(part, pl.BlockSpec((CHUNK + BITS, 2 * TILE), lambda t, *_: (0, 0))) for part in parts]
    inputs += [(part, units) for part in first_parts]
    after, aliases = (), {}
    if before:
        tiles, other, scales = before
        inputs.append((scales, small))
        after, aliases = (tiles,), {7: 0}
        if chunk != LAST:
            after, aliases = (tiles, other), {7: 0, 8: 1}
    tile = (CHUNK, TILE)
    return call(
        kernel,
        (1,),
        [place, denominator],
        inputs,
        [
            ((2 * ROWS, TILE), jnp.bfloat16, pl.BlockSpec(tile, lambda t, p, d: (p[CORE] * CHUNKS + chunk, 0))),
            ((chunks * CHUNK, TILE), jnp.bfloat16, pl.BlockSpec(tile, lambda t, *_: (row0, 0))),
            ((8, 8), jnp.float32, small),
        ],
        after,
        [pltpu.VMEM((2, CHUNK, TILE), jnp.float32), pltpu.VMEM((2 * per_half, BLOCK), jnp.float32)],
        aliases,
    )


def assemble(place, tiles, came, scales, scales_came):
    def kernel(place, tiles_in, came, last_came, scales, scales_came, tiles, all_scales, sems):
        core = place[CORE]
        copies, first = [], 0
        for at, part in enumerate((came, last_came)):
            rows = pl.ds(pl.multiple_of((1 - core) * ROWS + first, CHUNK), part.shape[0])
            copies.append(pltpu.make_async_copy(part, tiles.at[rows, :], sems.at[at]))
            first += part.shape[0]
        for copy in copies:
            copy.start()
        for mine in range(2):

            @pl.when(core == mine)
            def _():
                cols = slice(4 * mine, 4 * mine + 4)
                all_scales[8 * mine : 8 * mine + 8, :] = scales[:, cols]
                all_scales[8 - 8 * mine : 16 - 8 * mine, :] = scales_came[:, cols]

        for copy in copies:
            copy.wait()

    vmem = pl.BlockSpec(memory_space=pltpu.VMEM)
    return call(
        kernel,
        (),
        [place],
        [(tiles, ANYWHERE), *[(part, ANYWHERE) for part in came], (scales, vmem), (scales_came, vmem)],
        [((2 * ROWS, TILE), jnp.bfloat16, ANYWHERE), ((16, 4), jnp.float32, vmem)],
        (),
        [pltpu.SemaphoreType.DMA((2,))],
        {1: 0},
    )


def body(quant_codes, exponents, numerators, denominator):
    y_hi, x = jnp.divmod(lax.axis_index("ckpt"), 4)
    row = lax.axis_index("row")
    z, core = (row // 2) % 4, row % 2
    keep = (x + core) % 2
    place = jnp.stack(
        [y_hi * 4 + x, y_hi * 4 + (x + 1 - 2 * keep) % 4, keep, y_hi, ((z - x) % 4) // 2, core]
    ).astype(jnp.int32)
    wide_exps = jnp.pad(jnp.repeat(exponents[0], BLOCK, axis=1), ((0, UNITS - 8), (0, 0))).astype(
        jnp.bfloat16
    )

    def swap_pairs(chunk, after):
        return lax.ppermute(pack(chunk, place, quant_codes, wide_exps, after), AXES, PAIR_PERM)

    def pairs_of(chunk, after):
        return add_pairs(
            chunk, place, numerators, wide_exps, quant_codes, received[0], received[chunk], after
        )

    def move_y(pair, *after):
        far, near = later(pair, *after)
        return lax.ppermute(far, AXES, ACROSS_PERM), lax.ppermute(near, AXES, BESIDE_PERM)

    def fours_of(chunk, after):
        return add_fours(chunk, place, *moved[0], *moved[chunk], after)

    def move(pair, perms, *after):
        return [lax.ppermute(part, AXES, perm) for part, perm in zip(later(pair, *after), perms)]

    def finished(chunk, before):
        return finish(chunk, place, denominator, parts[0], parts[chunk], before)

    received, pairs, moved, fours, parts = {}, {}, {}, {}, {}
    received[0] = swap_pairs(0, ())
    received[1] = swap_pairs(1, ())
    pairs[0] = pairs_of(0, ())
    moved[0] = move_y(pairs[0])
    received[2] = swap_pairs(2, pairs[0])
    pairs[1] = pairs_of(1, pairs[0])
    fours[0] = fours_of(0, pairs[1])
    moved[1] = move_y(pairs[1], fours[0])
    received[3] = swap_pairs(3, (*pairs[1], *fours[0]))
    parts[0] = move(fours[0], Z_PERMS)
    pairs[2] = pairs_of(2, (*pairs[1], *fours[0]))
    fours[1] = fours_of(1, pairs[2])
    moved[2] = move_y(pairs[2], fours[1])
    parts[1] = move(fours[1], Z_PERMS, parts[0])
    pairs[3] = pairs_of(3, (*fours[1], *parts[0]))
    parts[0] = move(parts[0], X_PERMS, received[3])
    fours[2] = fours_of(2, pairs[3])
    moved[3] = move_y(pairs[3], fours[2])
    parts[2] = move(fours[2], Z_PERMS, parts[1])
    parts[1] = move(parts[1], X_PERMS, parts[0])
    done = finished(0, None)
    done = finished(1, done)
    fours[3] = fours_of(3, tuple(done))
    parts[3] = move(fours[3], Z_PERMS, parts[2])
    parts[2] = move(parts[2], X_PERMS, parts[1])
    parts[3] = move(parts[3], X_PERMS)
    done = finished(2, done)
    came = lax.ppermute(done[1], AXES, CORE_PERM)
    tiles, other, scales = finished(3, done)
    last_came = lax.ppermute(other, AXES, CORE_PERM)
    scales_came = lax.ppermute(scales, AXES, CORE_PERM)
    return tuple(assemble(place, tiles, (came, last_came), scales, scales_came))


def solution(mesh):
    placed = (P("ckpt", "row", None), P("ckpt", "row", None), P(), P())
    return jax.shard_map(
        body,
        mesh=mesh,
        in_specs=placed,
        out_specs=(P("ckpt", "row"), P("ckpt", "row")),
        check_vma=False,
    )
```

```python
import jax
import jax.numpy as jnp
from jax import lax
from jax.experimental import pallas as pl
from jax.experimental.pallas import tpu as pltpu
from jax.sharding import PartitionSpec as P

BLOCK = 128
EPSILON = 1e-6
AXES = ("ckpt", "row")
OWN, PARTNER, KEEP, YHI, SLOT, CORE = range(6)
TILE = 512
WIDTH = 1024
ROWS = 1024
CHUNK = 256
CHUNKS = ROWS // CHUNK
BANDS = CHUNK // BLOCK
BITS = CHUNK // 16
LAST = CHUNKS - 1
UNITS = 16


def device_index(x, y, z, core):
    y_hi, y_lo = divmod(y, 2)
    return (y_hi * 4 + x) * 16 + y_lo * 8 + z * 2 + core


def permutation(target):
    return [
        (device_index(x, y, z, core), device_index(*target(x, y, z, core)))
        for x in range(4)
        for y in range(4)
        for z in range(4)
        for core in range(2)
    ]


def pair_of(x, y, z, core):
    return (x + 1 - 2 * ((x + core) % 2)) % 4, y, z, core


def z_target(m, x, y, z, core):
    away = (z - x) % 4
    return x, y, (x + core) % 2 + 2 * (m ^ (away // 2)), away % 2


def x_target(m, x, y, z, core):
    return (x + core + 2 * (m ^ (z // 2))) % 4, y, z, (z - x) % 2


ACROSS = {0: 1, 1: 3, 2: 0, 3: 2}
BESIDE = {0: 0, 1: 2, 2: 1, 3: 3}
PAIR_PERM = permutation(pair_of)
ACROSS_PERM = permutation(lambda x, y, z, core: (x, ACROSS[y], z, core))
BESIDE_PERM = permutation(lambda x, y, z, core: (x, BESIDE[y], z, core))
Z_PERMS = [permutation(lambda *at, m=m: z_target(m, *at)) for m in range(2)]
X_PERMS = [permutation(lambda *at, m=m: x_target(m, *at)) for m in range(2)]
CORE_PERM = permutation(lambda x, y, z, core: (x, y, z, 1 - core))


def call(kernel, grid, scalars, inputs, outputs, after=(), scratch=(), aliases=None):
    first = len(scalars) + len(inputs)

    def whole(*refs):
        kernel(*refs[:first], *refs[first + len(after) :])

    moved = sum(a.dtype.itemsize * a.size for a, _ in inputs)
    return pl.pallas_call(
        whole,
        grid_spec=pltpu.PrefetchScalarGridSpec(
            num_scalar_prefetch=len(scalars),
            grid=grid,
            in_specs=[spec for _, spec in inputs] + [pl.BlockSpec(memory_space=pl.ANY)] * len(after),
            out_specs=[spec for _, _, spec in outputs],
            scratch_shapes=scratch,
        ),
        out_shape=[jax.ShapeDtypeStruct(s, d) for s, d, _ in outputs],
        input_output_aliases=aliases or {},
        compiler_params=pltpu.CompilerParams(vmem_limit_bytes=40 * 1024 * 1024),
        cost_estimate=pl.CostEstimate(flops=0, bytes_accessed=moved, transcendentals=0),
    )(*scalars, *[a for a, _ in inputs], *after)


def later(values, *after):
    return lax.optimization_barrier((tuple(values), after))[0] if after else values


ANYWHERE = pl.BlockSpec(memory_space=pl.ANY)


def pack(chunk, place, codes, wide_exps, after):
    extra = UNITS if chunk == 0 else 0

    def kernel(place, codes, wide_exps, sent, sems):
        copies = []
        for group in range(4):
            y_lo, t = divmod(group, 2)
            first = pl.multiple_of((y_lo * 4 + 1 - place[KEEP] + 2 * t) * 2 * TILE, BLOCK)
            cols, to = pl.ds(first, 2 * TILE), pl.ds(group * 2 * TILE, 2 * TILE)
            copies.append(
                pltpu.make_async_copy(
                    codes.at[0, pl.ds(chunk * CHUNK, CHUNK), cols],
                    sent.at[pl.ds(0, CHUNK), to],
                    sems.at[group],
                )
            )
            if extra:
                copies.append(
                    pltpu.make_async_copy(
                        wide_exps.at[:, cols], sent.at[pl.ds(CHUNK, UNITS), to], sems.at[4 + group]
                    )
                )
        for copy in copies:
            copy.start()
        for copy in copies:
            copy.wait()

    return call(
        kernel,
        (),
        [place],
        [(codes, ANYWHERE), (wide_exps, ANYWHERE)],
        [((CHUNK + extra, 8 * TILE), jnp.bfloat16, ANYWHERE)],
        after,
        [pltpu.SemaphoreType.DMA((8,))],
    )[0]


def whole_number(ref):
    return ref[...].astype(jnp.float32).astype(jnp.int32)


def add_pairs(chunk, place, weights, wide_exps, codes, first_received, received, after):
    extra = UNITS if chunk == 0 else 0

    def kernel(place, weights, *refs):
        own_weight, partner_weight = weights[place[OWN]], weights[place[PARTNER]]
        for at in range(2):
            kept, came, own, partner, out = refs[at::2]
            own, partner = whole_number(own), whole_number(partner)
            unit = jnp.minimum(own, partner)
            own = (jnp.full(own.shape, own_weight, jnp.int32) << (own - unit)).astype(jnp.float32)
            partner = (jnp.full(own.shape, partner_weight, jnp.int32) << (partner - unit)).astype(
                jnp.float32
            )
            for band in range(BANDS):
                row = chunk * BANDS + band
                rows = pl.ds(band * BLOCK, BLOCK)
                for col in range(WIDTH // BLOCK):
                    cols = slice(col * BLOCK, (col + 1) * BLOCK)
                    total = (
                        kept[0, rows, cols].astype(jnp.float32) * own[row : row + 1, cols]
                        + came[rows, cols].astype(jnp.float32) * partner[row : row + 1, cols]
                    )
                    out[rows, cols] = total.astype(jnp.int32).astype(jnp.int16)
            if extra:
                out[pl.ds(CHUNK, UNITS), :] = unit.astype(jnp.int16)

    far, near = (lambda p: 1 - p[YHI]), (lambda p: p[YHI])

    def kept_at(y_lo, row):
        return lambda t, p, w: (*row, y_lo(p) * 4 + p[KEEP] + 2 * t)

    def came_at(y_lo, row):
        return lambda t, p, w: (row, y_lo(p) * 2 + t)

    sent = (CHUNK + extra, WIDTH)
    return call(
        kernel,
        (2,),
        [place, weights],
        [(codes, pl.BlockSpec((1, CHUNK, WIDTH), kept_at(y, (0, chunk)))) for y in (far, near)]
        + [(received, pl.BlockSpec((CHUNK, WIDTH), came_at(y, 0))) for y in (far, near)]
        + [(wide_exps, pl.BlockSpec((UNITS, WIDTH), kept_at(y, (0,)))) for y in (far, near)]
        + [(first_received, pl.BlockSpec((UNITS, WIDTH), came_at(y, CHUNK // UNITS))) for y in (far, near)],
        [((CHUNK + extra, 4 * TILE), jnp.int16, pl.BlockSpec(sent, lambda t, *_: (0, t)))] * 2,
        after,
    )


def add_fours(chunk, place, first_far, first_near, far, near, after):
    extra = UNITS if chunk == 0 else 0

    def kernel(place, far, near, far_unit, near_unit, *outs):
        far_unit, near_unit = far_unit[...].astype(jnp.int32), near_unit[...].astype(jnp.int32)
        unit = jnp.minimum(far_unit, near_unit)
        far_unit, near_unit = far_unit - unit, near_unit - unit

        def fill(out):
            for col in range(2 * TILE // BLOCK):
                cols = slice(col * BLOCK, (col + 1) * BLOCK)
                odds = []
                for band in range(BANDS):
                    row = chunk * BANDS + band
                    rows = pl.ds(band * BLOCK, BLOCK)
                    total = (
                        far[rows, cols].astype(jnp.int32)
                        << jnp.broadcast_to(far_unit[row : row + 1, cols], (BLOCK, BLOCK))
                    ) + (
                        near[rows, cols].astype(jnp.int32)
                        << jnp.broadcast_to(near_unit[row : row + 1, cols], (BLOCK, BLOCK))
                    )
                    out[rows, cols] = (total >> 1).astype(jnp.int16)
                    odd = total & 1
                    packed = odd[0:8]
                    for group in range(1, 16):
                        packed = packed | (odd[8 * group : 8 * group + 8] << group)
                    odds.append(packed)
                out[pl.ds(CHUNK, BITS), cols] = jnp.concatenate(odds, axis=0).astype(jnp.int16)
            if extra:
                out[pl.ds(CHUNK + BITS, UNITS), :] = unit.astype(jnp.int16)

        for slot, out in enumerate(outs):
            pl.when(pl.program_id(0) == slot)(lambda out=out: fill(out))

    rows = CHUNK + BITS + extra
    picked = lambda t, p: jnp.bitwise_xor(t, p[SLOT])
    block = pl.BlockSpec((CHUNK, 2 * TILE), lambda t, p: (0, picked(t, p)))
    units = pl.BlockSpec((UNITS, 2 * TILE), lambda t, p: (CHUNK // UNITS, picked(t, p)))
    return call(
        kernel,
        (2,),
        [place],
        [(far, block), (near, block), (first_far, units), (first_near, units)],
        [((rows, 2 * TILE), jnp.int16, pl.BlockSpec((rows, 2 * TILE), lambda t, p: (0, 0)))] * 2,
        after,
    )


def finish(chunk, place, denominator, first_parts, parts, before):
    chunks, row0 = (1, 0) if chunk == LAST else (CHUNKS - 1, chunk)
    per_half = BANDS * (TILE // BLOCK)

    def kernel(place, denominator, *refs):
        parts, units = refs[:2], refs[2:4]
        old_scales = refs[4] if before else None
        mine, other, scales, summed, factors = refs[-5:]
        core = place[CORE]
        divisor = jnp.full((1, 1), denominator[0], jnp.int32).astype(jnp.float32)
        units = [
            (1 << (unit[...].astype(jnp.int32) + 8)).astype(jnp.float32) * (1.0 / 256) for unit in units
        ]

        def fours(ref, unit, band, cols):
            packed = ref[pl.ds(CHUNK, BITS), cols].astype(jnp.int32)[8 * band : 8 * band + 8]
            odd = jnp.concatenate([(packed >> group) & 1 for group in range(16)], axis=0)
            total = (ref[pl.ds(band * BLOCK, BLOCK), cols].astype(jnp.int32) << 1) + odd
            row = chunk * BANDS + band
            return total.astype(jnp.float32) * unit[row : row + 1, cols]

        blocks = [(h, band, col) for h in range(2) for band in range(BANDS) for col in range(TILE // BLOCK)]
        tops = []
        for half, band, col in blocks:
            cols = slice(half * TILE + col * BLOCK, half * TILE + (col + 1) * BLOCK)
            total = fours(parts[0], units[0], band, cols) + fours(parts[1], units[1], band, cols)
            summed[half, pl.ds(band * BLOCK, BLOCK), col * BLOCK : (col + 1) * BLOCK] = total
            tops.append(jnp.max(jnp.abs(total), axis=0, keepdims=True))
        scale = jnp.max(jnp.concatenate(tops, axis=0), axis=1, keepdims=True) / divisor
        factors[...] = jnp.broadcast_to(1.0 / (divisor * (scale + EPSILON)), factors.shape)
        found = old_scales[...] if before else jnp.zeros_like(scales)
        row_at = lax.broadcasted_iota(jnp.int32, scales.shape, 0)
        col_at = lax.broadcasted_iota(jnp.int32, scales.shape, 1)
        for at, (half, band, col) in enumerate(blocks):
            here = (row_at == chunk * BANDS + band) & (col_at == half * (TILE // BLOCK) + col)
            found = jnp.where(here, scale[at : at + 1, :], found)
        scales[...] = found
        for half, out in ((core, mine), (1 - core, other)):
            for at in range(per_half):
                band, col = divmod(at, TILE // BLOCK)
                rows, cols = pl.ds(band * BLOCK, BLOCK), slice(col * BLOCK, (col + 1) * BLOCK)
                factor = factors[pl.ds(half * per_half + at, 1), :]
                out[rows, cols] = (summed[half, rows, cols] * factor).astype(jnp.bfloat16)

    small = pl.BlockSpec((8, 8), lambda t, *_: (0, 0))
    units = pl.BlockSpec((UNITS, 2 * TILE), lambda t, *_: ((CHUNK + BITS) // UNITS, 0))
    inputs = [(part, pl.BlockSpec((CHUNK + BITS, 2 * TILE), lambda t, *_: (0, 0))) for part in parts]
    inputs += [(part, units) for part in first_parts]
    after, aliases = (), {}
    if before:
        tiles, other, scales = before
        inputs.append((scales, small))
        after, aliases = (tiles,), {7: 0}
        if chunk != LAST:
            after, aliases = (tiles, other), {7: 0, 8: 1}
    tile = (CHUNK, TILE)
    return call(
        kernel,
        (1,),
        [place, denominator],
        inputs,
        [
            ((2 * ROWS, TILE), jnp.bfloat16, pl.BlockSpec(tile, lambda t, p, d: (p[CORE] * CHUNKS + chunk, 0))),
            ((chunks * CHUNK, TILE), jnp.bfloat16, pl.BlockSpec(tile, lambda t, *_: (row0, 0))),
            ((8, 8), jnp.float32, small),
        ],
        after,
        [pltpu.VMEM((2, CHUNK, TILE), jnp.float32), pltpu.VMEM((2 * per_half, BLOCK), jnp.float32)],
        aliases,
    )


def assemble(place, tiles, came, scales, scales_came):
    def kernel(place, tiles_in, came, last_came, scales, scales_came, tiles, all_scales, sems):
        core = place[CORE]
        copies, first = [], 0
        for at, part in enumerate((came, last_came)):
            rows = pl.ds(pl.multiple_of((1 - core) * ROWS + first, CHUNK), part.shape[0])
            copies.append(pltpu.make_async_copy(part, tiles.at[rows, :], sems.at[at]))
            first += part.shape[0]
        for copy in copies:
            copy.start()
        for mine in range(2):

            @pl.when(core == mine)
            def _():
                cols = slice(4 * mine, 4 * mine + 4)
                all_scales[8 * mine : 8 * mine + 8, :] = scales[:, cols]
                all_scales[8 - 8 * mine : 16 - 8 * mine, :] = scales_came[:, cols]

        for copy in copies:
            copy.wait()

    vmem = pl.BlockSpec(memory_space=pltpu.VMEM)
    return call(
        kernel,
        (),
        [place],
        [(tiles, ANYWHERE), *[(part, ANYWHERE) for part in came], (scales, vmem), (scales_came, vmem)],
        [((2 * ROWS, TILE), jnp.bfloat16, ANYWHERE), ((16, 4), jnp.float32, vmem)],
        (),
        [pltpu.SemaphoreType.DMA((2,))],
        {1: 0},
    )


def body(quant_codes, exponents, numerators, denominator):
    y_hi, x = jnp.divmod(lax.axis_index("ckpt"), 4)
    row = lax.axis_index("row")
    z, core = (row // 2) % 4, row % 2
    keep = (x + core) % 2
    place = jnp.stack(
        [y_hi * 4 + x, y_hi * 4 + (x + 1 - 2 * keep) % 4, keep, y_hi, ((z - x) % 4) // 2, core]
    ).astype(jnp.int32)
    wide_exps = jnp.pad(jnp.repeat(exponents[0], BLOCK, axis=1), ((0, UNITS - 8), (0, 0))).astype(
        jnp.bfloat16
    )

    def swap_pairs(chunk, after):
        return lax.ppermute(pack(chunk, place, quant_codes, wide_exps, after), AXES, PAIR_PERM)

    def pairs_of(chunk, after):
        return add_pairs(
            chunk, place, numerators, wide_exps, quant_codes, received[0], received[chunk], after
        )

    def move_y(pair, *after):
        far, near = later(pair, *after)
        return lax.ppermute(far, AXES, ACROSS_PERM), lax.ppermute(near, AXES, BESIDE_PERM)

    def fours_of(chunk, after):
        return add_fours(chunk, place, *moved[0], *moved[chunk], after)

    def move(pair, perms, *after):
        return [lax.ppermute(part, AXES, perm) for part, perm in zip(later(pair, *after), perms)]

    def finished(chunk, before):
        return finish(chunk, place, denominator, parts[0], parts[chunk], before)

    received, pairs, moved, fours, parts = {}, {}, {}, {}, {}
    received[0] = swap_pairs(0, ())
    received[1] = swap_pairs(1, ())
    pairs[0] = pairs_of(0, ())
    moved[0] = move_y(pairs[0])
    received[2] = swap_pairs(2, pairs[0])
    pairs[1] = pairs_of(1, pairs[0])
    fours[0] = fours_of(0, pairs[1])
    moved[1] = move_y(pairs[1], fours[0])
    received[3] = swap_pairs(3, (*pairs[1], *fours[0]))
    parts[0] = move(fours[0], Z_PERMS)
    pairs[2] = pairs_of(2, (*pairs[1], *fours[0]))
    fours[1] = fours_of(1, pairs[2])
    moved[2] = move_y(pairs[2], fours[1])
    parts[1] = move(fours[1], Z_PERMS, parts[0])
    pairs[3] = pairs_of(3, (*fours[1], *parts[0]))
    parts[0] = move(parts[0], X_PERMS, pairs[3])
    fours[2] = fours_of(2, pairs[3])
    moved[3] = move_y(pairs[3], fours[2])
    parts[2] = move(fours[2], Z_PERMS, parts[1])
    parts[1] = move(parts[1], X_PERMS, parts[0])
    done = finished(0, None)
    done = finished(1, done)
    fours[3] = fours_of(3, tuple(done))
    parts[3] = move(fours[3], Z_PERMS, parts[2])
    parts[2] = move(parts[2], X_PERMS, parts[1])
    parts[3] = move(parts[3], X_PERMS)
    done = finished(2, done)
    came = lax.ppermute(done[1], AXES, CORE_PERM)
    tiles, other, scales = finished(3, done)
    last_came = lax.ppermute(other, AXES, CORE_PERM)
    scales_came = lax.ppermute(scales, AXES, CORE_PERM)
    return tuple(assemble(place, tiles, (came, last_came), scales, scales_came))


def solution(mesh):
    placed = (P("ckpt", "row", None), P("ckpt", "row", None), P(), P())
    return jax.shard_map(
        body,
        mesh=mesh,
        in_specs=placed,
        out_specs=(P("ckpt", "row"), P("ckpt", "row")),
        check_vma=False,
    )
```
